32 devices in a mesh: clip: 2 (over x), frame: 16 (over z, y, core).
Axes of the slice: x: 2, y: 2, z: 4, core: 2. Of those that a mesh axis runs over, the one named last changes fastest.
Arguments:
- feature_map: bfloat16 [32, 16320, 128], P(('clip', 'frame')), parts along dimension 0, may hold values from -4 to 4
- queries: bfloat16 [512, 128], P(('clip', 'frame')), parts along dimension 0, may hold values from -8 to 8
- corner: int32 [32, 256], P(('clip', 'frame')), parts along dimension 0, may hold values from 0 to 16198, as said below
- offsets: float32 [32, 2, 256], P(('clip', 'frame')), parts along dimension 0, may hold values from 0 to 1
- visible: int32 [32, 256], P(('clip', 'frame')), parts along dimension 0, may hold values 0 or 1
- w_embed: bfloat16 [256, 384], replicated, may hold values from -0.375 to 0.375
- w_qkv: bfloat16 [384, 1152], replicated, may hold values from -0.3125 to 0.3125
- w_out: bfloat16 [384, 384], replicated, may hold values from -0.3125 to 0.3125
- gain_attn: float32 [384], replicated, may hold values from 0.1 to 1.9
- gain_mlp: float32 [384], replicated, may hold values from 0.1 to 1.9
- w_up: bfloat16 [384, 1536], replicated, may hold values from -0.3125 to 0.3125
- w_down: bfloat16 [1536, 384], replicated, may hold values from -0.15625 to 0.15625
- w_head: bfloat16 [384, 128], replicated, may hold values from -0.3125 to 0.3125
Outputs:
- update: bfloat16 [32, 256, 128], P(('clip', 'frame')), parts along dimension 0
The draws below stay inside these ranges and needn't reach their ends.
There are 2 independent parts, one for each index of `clip`. The reference program is written for one: setup_inputs(seed, part) draws one part's arguments, and reference() takes and returns one part's arrays. A program takes and returns all parts, laid end to end along the dimension named above; an argument that names none is the same for every part. Nothing has to cross between parts.
Inputs may be any that keep to these rules, and one draw needn't show every extreme that they name: `corner`: each entry is the cell index of a cell that is not in the last row or the last column of the 136 x 120 grid.
All inputs are finite; a program needn't handle non-finite values. No bound on the sum of `visible` on one device may be relied on, other than what follows from the above.
Results may differ from the reference program's by a relative error of at most 0.009.
Values may be sent and summed in bfloat16 or wider, within the bound.
A program may use at most 64 MiB of HBM per device.

```python
import math
import jax
import jax.numpy as jnp
from jax import lax

C = 128
D = 384
FF = 1536
HEADS = 8
GRID_H = 136
GRID_W = 120
CELLS = 16320
FRAMES = 16
TRK = 256


def directions_for(key):
    proto_count = max(1, min(TRK, CELLS // 8))
    sign_key, size_key = jax.random.split(key)
    signs = jnp.where(jax.random.bernoulli(sign_key, 0.5, (proto_count, C)), 1.0, -1.0)
    sizes = jax.random.uniform(size_key, (proto_count, C), jnp.float32, 0.85, 1.15)
    return signs * sizes


def frame_places(one_key, proto_count):
    return jax.random.permutation(one_key, CELLS)[:3 * proto_count]


def draw_feature_map(key, part):
    directions = directions_for(key)
    proto_count = directions.shape[0]
    key = jax.random.fold_in(key, 11)
    base_key, scale_key, place_key, strength_key, noise_key = jax.random.split(key, 5)
    spread = jnp.exp(jax.random.uniform(scale_key, (FRAMES, CELLS, 1), jnp.float32, math.log(0.5), math.log(2.0)))
    background = jnp.clip(jax.random.normal(base_key, (FRAMES, CELLS, C), jnp.float32), -4.0, 4.0)
    strengths = jax.random.uniform(strength_key, (FRAMES, 3, proto_count), jnp.float32, 1.0, 2.6)
    background = jnp.clip(background * spread, -4.0, 4.0)
    frame_keys = jax.random.split(place_key, FRAMES)
    places = jax.vmap(partial_places(proto_count))(frame_keys).reshape(FRAMES, 3, proto_count)
    half_width = C // 2
    jitter = jnp.clip(jax.random.normal(noise_key, (FRAMES, 3, proto_count, half_width), jnp.float32), -2.0, 2.0)
    sideways = jnp.concatenate([jitter * directions[:, half_width:], -jitter * directions[:, :half_width]], axis=-1)
    planted = jnp.clip(strengths[..., None] * directions + 0.35 * sideways, -4.0, 4.0)
    frame_index = jnp.broadcast_to(jnp.arange(FRAMES)[:, None, None], places.shape)
    background = background.at[frame_index, places].set(planted)
    return background.astype(jnp.bfloat16)


def partial_places(proto_count):

    def chosen_places(one_key):
        return frame_places(one_key, proto_count)
    return chosen_places


def draw_queries(key, part):
    directions = directions_for(key)
    proto_count = directions.shape[0]
    key = jax.random.fold_in(key, 12)
    strength_key = jax.random.fold_in(key, 0)
    noise_key = jax.random.fold_in(key, 3)
    strengths = jnp.exp(jax.random.uniform(strength_key, (TRK,), jnp.float32, math.log(0.6), math.log(1.5)))
    chosen = directions[jnp.arange(TRK) % proto_count]
    jitter = jnp.clip(jax.random.normal(noise_key, (TRK, C), jnp.float32), -3.0, 3.0)
    base = jnp.clip(strengths[:, None] * chosen + 0.3 * jitter, -8.0, 8.0)
    return base.astype(jnp.bfloat16)


def draw_corner(key, part):
    key = jax.random.fold_in(key, 13)
    row_key, column_key = jax.random.split(key)
    grid_rows = jax.random.randint(row_key, (FRAMES, TRK), 0, GRID_H - 1)
    grid_columns = jax.random.randint(column_key, (FRAMES, TRK), 0, GRID_W - 1)
    places = grid_rows * GRID_W + grid_columns
    places = places.at[0, 0].set(CELLS - GRID_W - 2)
    places = places.at[0, 1].set(0)
    return places.astype(jnp.int32)


def plant(values, own_key, smallest, high):
    place = [jax.random.randint(jax.random.fold_in(own_key, axis), (), 0, length) for axis, length in enumerate(values.shape)]
    main_axis = values.shape.index(max(values.shape))
    beside = place[:main_axis] + [(place[main_axis] + 1) % values.shape[main_axis]] + place[main_axis + 1:]
    return values.at[tuple(place)].set(smallest).at[tuple(beside)].set(high)


def block_levels(rng, shape, cuts, low, high):
    level = 1.0
    for position, parts in cuts:
        heights = jax.random.uniform(jax.random.fold_in(jax.random.fold_in(rng, 6), position), (parts,), jnp.float32, low / len(cuts), high / len(cuts))
        level = level * jnp.repeat(jnp.exp(heights), shape[position] // parts).reshape((-1,) + (1,) * (len(shape) - 1 - position))
    return level


def bell_draw(stream_key, shape, deviation, limit, kind=jnp.bfloat16):
    return jnp.clip(deviation * jax.random.normal(stream_key, shape, jnp.float32), -limit, limit).astype(kind)


def setup_inputs(seed: int = 0, part: int = 0) -> dict:
    key_of = jax.random.split(jax.random.key(seed), 14)
    part_keys = jax.random.split(jax.random.fold_in(key_of[13], part), 14)
    return {
        "feature_map": draw_feature_map(jax.random.fold_in(jax.random.fold_in(key_of[13], part), 71), part),
        "queries": draw_queries(jax.random.fold_in(jax.random.fold_in(key_of[13], part), 71), part),
        "corner": draw_corner(jax.random.fold_in(jax.random.fold_in(key_of[13], part), 71), part),
        "offsets": jnp.clip(1.0 * jax.random.uniform(part_keys[3], (FRAMES, 2, TRK), jnp.float32) ** block_levels(part_keys[3], (FRAMES, 2, TRK), ((0, 16),), -0.2, 0.2), 0.0, 1.0),
        "visible": plant((jax.random.randint(part_keys[4], (FRAMES, TRK), 0, 4) < 3).astype(jnp.int32), jax.random.fold_in(part_keys[4], 1), 0, 1),
        "w_embed": bell_draw(key_of[5], (2 * C, D), (2 * C) ** -0.5, 0.375),
        "w_qkv": bell_draw(key_of[6], (D, 3 * D), D ** -0.5, 0.3125),
        "w_out": bell_draw(key_of[7], (D, D), D ** -0.5, 0.3125),
        "gain_attn": jnp.clip(1.0 + 0.18 * jax.random.normal(key_of[8], (D,), jnp.float32), 0.1, 1.9),
        "gain_mlp": jnp.clip(1.0 + 0.18 * jax.random.normal(key_of[9], (D,), jnp.float32), 0.1, 1.9),
        "w_up": bell_draw(key_of[10], (D, FF), D ** -0.5, 0.3125),
        "w_down": bell_draw(key_of[11], (FF, D), FF ** -0.5, 0.15625),
        "w_head": bell_draw(key_of[12], (D, C), D ** -0.5, 0.3125),
    }


def sample(frame_map, idx, frac):
    across = frac[0]
    upward = frac[1]
    weights = jnp.stack([(1.0 - across) * (1.0 - upward), across * (1.0 - upward), (1.0 - across) * upward, across * upward])
    places = jnp.stack([idx, idx + 1, idx + GRID_W, idx + GRID_W + 1]).astype(jnp.int32)
    corner_rows = jnp.take(frame_map, places, axis=0).astype(jnp.float32)
    return lax.optimization_barrier(jnp.sum(corner_rows * weights[:, :, None], axis=0)).astype(jnp.bfloat16)

def correlate(frame_map, query_rows):
    count = query_rows.shape[0]
    width = query_rows.shape[1]
    block_rows = math.gcd(count, 256)
    blocks = query_rows.reshape(count // block_rows, block_rows, width)
    scale = 1.0 / math.sqrt(width)

    def single(block):
        scores = lax.dot_general(block, frame_map, (((1,), (1,)), ((), ())), preferred_element_type=jnp.float32) * scale
        probs = jax.nn.softmax(scores, axis=-1).astype(jnp.bfloat16)
        return jnp.dot(probs, frame_map, preferred_element_type=jnp.float32).astype(jnp.bfloat16)
    return lax.map(single, blocks).reshape(count, width)

def rms_scale(values, gain):
    return values * lax.rsqrt(lax.optimization_barrier(jnp.mean(values * values, axis=-1, keepdims=True)) + 1e-06) * gain

def temporal(stream, allowed, w_qkv, w_out, gain_attn, gain_mlp, w_up, w_down, w_head):
    frames = stream.shape[0]
    count = stream.shape[1]
    width = stream.shape[2]
    head_size = width // HEADS
    flowing = stream.astype(jnp.float32)
    normed = rms_scale(flowing, gain_attn).astype(jnp.bfloat16)
    packed = jnp.dot(normed, w_qkv, preferred_element_type=jnp.float32).astype(jnp.bfloat16)
    queries_h = packed[:, :, :width].reshape(frames, count, HEADS, head_size)
    keys_h = packed[:, :, width:2 * width].reshape(frames, count, HEADS, head_size)
    values_h = packed[:, :, 2 * width:].reshape(frames, count, HEADS, head_size)
    scores = jnp.einsum('fnhe,gnhe->nhfg', queries_h.astype(jnp.float32), keys_h.astype(jnp.float32)) / math.sqrt(head_size)
    diagonal = jnp.eye(frames, dtype=bool)
    keep = jnp.logical_or(jnp.transpose(allowed)[:, None, :], diagonal[None, :, :])
    scores = jnp.where(keep[:, None, :, :], scores, jnp.float32(-1e+30))
    attn = jax.nn.softmax(scores, axis=-1).astype(jnp.bfloat16)
    context = jnp.einsum('nhfg,gnhe->fnhe', attn.astype(jnp.float32), values_h.astype(jnp.float32))
    context = context.astype(jnp.bfloat16).reshape(frames, count, width)
    mixed = flowing + jnp.dot(context, w_out, preferred_element_type=jnp.float32)
    normed_mlp = rms_scale(mixed, gain_mlp).astype(jnp.bfloat16)
    hidden = jax.nn.gelu(jnp.dot(normed_mlp, w_up, preferred_element_type=jnp.float32)).astype(jnp.bfloat16)
    final = (mixed + jnp.dot(hidden, w_down, preferred_element_type=jnp.float32)).astype(jnp.bfloat16)
    return jnp.dot(final, w_head, preferred_element_type=jnp.float32).astype(jnp.bfloat16)

def reference(feature_map, queries, corner, offsets, visible, w_embed, w_qkv, w_out, gain_attn, gain_mlp, w_up, w_down, w_head):

    def per_frame(items):
        frame_map, idx, frac = items
        return jnp.concatenate([sample(frame_map, idx, frac), correlate(frame_map, queries)], axis=-1)
    token_in = lax.map(per_frame, (feature_map, corner, offsets))
    stream = jnp.dot(token_in, w_embed, preferred_element_type=jnp.float32).astype(jnp.bfloat16)
    return temporal(stream, visible > 0, w_qkv, w_out, gain_attn, gain_mlp, w_up, w_down, w_head)
```

```python
import functools
import math

import jax
import jax.numpy as jnp
from jax import lax
from jax.experimental import pallas as pl
from jax.experimental.pallas import tpu as pltpu
from jax.sharding import PartitionSpec as P

HEADS = 8
GRID_W = 120
EPS = 1e-06
TILE = 16
WINDOW = 2 * TILE
GROUP = 8
MESH = pl.DeviceIdType.MESH
F32 = jnp.float32
BF16 = jnp.bfloat16


def pick_chunk(cells, limit):
    best = 16
    for rows in range(16, limit + 1, 16):
        if cells % rows == 0:
            best = rows
    return best


def each(count, step):
    if count == 1:
        step(0)
    else:

        def looped(i, carry):
            step(i)
            return carry

        lax.fori_loop(0, count, looped, 0)


def start_of(i, size):
    if isinstance(i, int):
        return i * size
    return pl.multiple_of(i * size, size)


def rms_scale(values, gain):
    return values * lax.rsqrt(jnp.mean(values * values, axis=-1, keepdims=True) + EPS) * gain


def dot(a, b):
    return jnp.dot(a, b, preferred_element_type=F32)


def dot_nt(a, b):
    return lax.dot_general(a, b, (((1,), (1,)), ((), ())), preferred_element_type=F32)


def dot_tn(a, b):
    return lax.dot_general(a, b, (((0,), (0,)), ((), ())), preferred_element_type=F32)


def kernel(
    n,
    fm_hbm,
    q_ref,
    tiles_s,
    corner_ref,
    off_ref,
    vis_ref,
    we_hbm,
    wqkv_hbm,
    wout_hbm,
    ga_ref,
    gm_ref,
    wup_hbm,
    wdown_hbm,
    whead_hbm,
    o_ref,
    fm,
    we,
    wqkv,
    wout,
    wup,
    wdown,
    whead,
    q_all,
    vis_all,
    table,
    tokens,
    outgoing,
    stream,
    packed,
    refined,
    returned,
    fm_sem,
    w_sem,
    q_send,
    q_recv,
    v_send,
    v_recv,
    s_send,
    s_recv,
    r_send,
    r_recv,
):
    chan = fm.shape[2]
    cells = fm.shape[0] * TILE
    tracks = q_all.shape[0]
    per = tracks // n
    rows = n * per
    width = stream.shape[1]
    me = lax.axis_index("frame")
    clip = lax.axis_index("clip")

    parts = fm_sem.shape[0]
    part_rows = fm.shape[0] // parts
    fm_copies = []
    for i in range(parts):
        piece = pl.ds(i * part_rows, part_rows)
        fm_copies.append(pltpu.make_async_copy(fm_hbm.at[piece], fm.at[piece], fm_sem.at[i]))
    for copy in fm_copies:
        copy.start()
    w_copies = [
        pltpu.make_async_copy(src, dst, w_sem.at[i])
        for i, (src, dst) in enumerate(
            [
                (we_hbm, we),
                (wqkv_hbm, wqkv),
                (wout_hbm, wout),
                (wup_hbm, wup),
                (wdown_hbm, wdown),
                (whead_hbm, whead),
            ]
        )
    ]
    for copy in w_copies:
        copy.start()

    def peer(k):
        return lax.rem(me + k, n)

    barrier = pltpu.get_barrier_semaphore()

    def greet(k, carry):
        pl.semaphore_signal(barrier, inc=1, device_id=(clip, peer(k)), device_id_type=MESH)
        return carry

    lax.fori_loop(1, n, greet, 0)
    pl.semaphore_wait(barrier, n - 1)

    mine = pl.ds(pl.multiple_of(me * per, per), per)

    def q_copy(k):
        return pltpu.make_async_remote_copy(
            src_ref=q_ref,
            dst_ref=q_all.at[mine],
            send_sem=q_send.at[k],
            recv_sem=q_recv.at[k],
            device_id=(clip, peer(k)),
            device_id_type=MESH,
        )

    def v_copy(k):
        return pltpu.make_async_remote_copy(
            src_ref=vis_ref,
            dst_ref=vis_all.at[me],
            send_sem=v_send.at[k],
            recv_sem=v_recv.at[k],
            device_id=(clip, peer(k)),
            device_id_type=MESH,
        )

    def s_copy(k):
        other = peer(k)
        return pltpu.make_async_remote_copy(
            src_ref=outgoing.at[pl.ds(pl.multiple_of(other * per, per), per)],
            dst_ref=stream.at[mine],
            send_sem=s_send.at[k],
            recv_sem=s_recv.at[k],
            device_id=(clip, other),
            device_id_type=MESH,
        )

    def r_copy(k):
        other = peer(k)
        return pltpu.make_async_remote_copy(
            src_ref=refined.at[pl.ds(pl.multiple_of(other * per, per), per)],
            dst_ref=returned.at[mine],
            send_sem=r_send.at[k],
            recv_sem=r_recv.at[k],
            device_id=(clip, other),
            device_id_type=MESH,
        )

    def over_peers(action):
        def step(k, carry):
            action(k)
            return carry

        lax.fori_loop(1, n, step, 0)

    over_peers(lambda k: q_copy(k).start())
    over_peers(lambda k: v_copy(k).start())
    q_all[mine, :] = q_ref[...]
    vis_all[me] = vis_ref[...]

    idx = corner_ref[...]
    ox = off_ref[0:1, :]
    oy = off_ref[1:2, :]
    table[...] = jnp.concatenate(
        [
            (idx % TILE).astype(F32),
            ((idx + GRID_W) % TILE + WINDOW).astype(F32),
            (1.0 - ox) * (1.0 - oy),
            ox * (1.0 - oy),
            (1.0 - ox) * oy,
            ox * oy,
            ox,
            oy,
        ],
        axis=0,
    ).T
    for copy in fm_copies:
        copy.wait()

    span = 2 * WINDOW
    lane = lax.broadcasted_iota(jnp.int32, (GROUP, GROUP * span), 1)
    own = lane // span == lax.broadcasted_iota(jnp.int32, (GROUP, GROUP * span), 0)
    within = jnp.where(own, lane % span, -2).astype(F32)

    def sample(g, carry):
        first = pl.multiple_of(g * GROUP, GROUP)
        pieces = []
        for t in range(GROUP):
            for i in range(4):
                pieces.append(fm[tiles_s[i, first + t]])
        window = jnp.concatenate(pieces, axis=0)
        facts = table[pl.ds(first, GROUP), :]
        p = facts[:, 0:1]
        r = facts[:, 1:2]
        zero = jnp.zeros_like(within)
        weight = jnp.where(within == p, facts[:, 2:3], zero)
        weight = jnp.where(within == p + 1.0, facts[:, 3:4], weight)
        weight = jnp.where(within == r, facts[:, 4:5], weight)
        weight = jnp.where(within == r + 1.0, facts[:, 5:6], weight)
        coarse = weight.astype(BF16)
        fine = (weight - coarse.astype(F32)).astype(BF16)
        both = dot(jnp.concatenate([coarse, fine], axis=0), window)
        tokens[pl.ds(first, GROUP), :] = both[:GROUP] + both[GROUP:]
        return carry

    lax.fori_loop(0, tracks // GROUP, sample, 0)

    over_peers(lambda k: q_copy(k).wait())

    block = math.gcd(tracks, 256)
    chunk = pick_chunk(cells, 1100)
    chunks = cells // chunk
    factor = math.log2(math.e) / math.sqrt(chan)
    w_copies[0].wait()

    def correlate(b):
        here = pl.ds(start_of(b, block), block)
        q = q_all[here, :]

        def piece_of(c):
            return fm[pl.ds(c * (chunk // TILE), chunk // TILE)].reshape(chunk, chan)

        def scores(c):
            return dot_nt(piece_of(c), q)

        ahead = scores(0)
        peak = total = acc = None
        for c in range(chunks):
            s = ahead
            if c + 1 < chunks:
                ahead = scores(c + 1)
            high = jnp.max(s, axis=0, keepdims=True)
            new = high if peak is None else jnp.maximum(peak, high)
            p = jnp.exp2(s * factor - new * factor)
            mass = jnp.sum(p, axis=0, keepdims=True)
            part = dot_tn(piece_of(c), p.astype(BF16))
            if peak is None:
                total, acc = mass, part
            else:
                shrink = jnp.exp2((peak - new) * factor)
                total = total * shrink + mass
                acc = acc * shrink + part
            peak = new
        pooled = (acc / total).T.astype(BF16)
        token = jnp.concatenate([tokens[here, :].astype(BF16), pooled], axis=1)
        outgoing[here, :] = dot(token, we[...]).astype(BF16)

    each(tracks // block, correlate)

    over_peers(lambda k: s_copy(k).start())
    stream[mine, :] = outgoing[mine, :]

    over_peers(lambda k: v_copy(k).wait())
    shown = vis_all[...].reshape(n, tracks).astype(F32).astype(BF16)
    tall = lax.broadcasted_iota(jnp.int32, (tracks, rows), 0)
    wide = lax.broadcasted_iota(jnp.int32, (tracks, rows), 1)
    pick = jnp.where(tall == me * per + wide % per, 1.0, 0.0).astype(BF16)
    frame_row = lax.broadcasted_iota(jnp.int32, (n, rows), 0)
    frame_col = lax.broadcasted_iota(jnp.int32, (n, rows), 1) // per
    seen = jnp.sum(
        jnp.where(frame_row == frame_col, dot(shown, pick), 0.0), axis=0, keepdims=True
    )
    for copy in w_copies[1:]:
        copy.wait()
    over_peers(lambda k: s_copy(k).wait())

    piece = math.gcd(rows, 256)

    def project(b):
        here = pl.ds(start_of(b, piece), piece)
        normed = rms_scale(stream[here, :].astype(F32), ga_ref[...]).astype(BF16)
        packed[here, :] = dot(normed, wqkv[...]).astype(BF16)

    each(rows // piece, project)

    size = width // HEADS

    def refine(b):
        first = start_of(b, piece)
        here = pl.ds(first, piece)
        q_row = lax.broadcasted_iota(jnp.int32, (piece, rows), 0) + first
        k_row = lax.broadcasted_iota(jnp.int32, (piece, rows), 1)
        same = q_row % per == k_row % per
        keep = jnp.logical_and(same, jnp.logical_or(q_row == k_row, seen > 0.5))
        bias = jnp.where(keep, 0.0, -1e30)
        tiles = [None] * (width // 128)
        for h in range(HEADS):
            lo = h * size // 128
            hi = -(-(h + 1) * size // 128)
            cols = lax.broadcasted_iota(jnp.int32, (1, (hi - lo) * 128), 1) + lo * 128
            inside = jnp.logical_and(cols >= h * size, cols < (h + 1) * size)
            gate = jnp.where(inside, 1.0, 0.0)
            qh = packed[here, lo * 128 : hi * 128] * gate.astype(BF16)
            kh = packed[:, width + lo * 128 : width + hi * 128]
            vh = packed[:, 2 * width + lo * 128 : 2 * width + hi * 128]
            s = dot_nt(qh, kh) * (1.0 / math.sqrt(size)) + bias
            p = jnp.exp(s - jnp.max(s, axis=1, keepdims=True))
            attn = (p / jnp.sum(p, axis=1, keepdims=True)).astype(BF16)
            got = dot(attn, vh) * gate
            for i in range(lo, hi):
                add = got[:, (i - lo) * 128 : (i - lo + 1) * 128]
                tiles[i] = add if tiles[i] is None else tiles[i] + add
        context = jnp.concatenate(tiles, axis=1).astype(BF16)
        mixed = stream[here, :].astype(F32) + dot(context, wout[...])
        normed = rms_scale(mixed, gm_ref[...]).astype(BF16)
        hidden = jax.nn.gelu(dot(normed, wup[...])).astype(BF16)
        final = (mixed + dot(hidden, wdown[...])).astype(BF16)
        refined[here, :] = dot(final, whead[...]).astype(BF16)

    each(rows // piece, refine)

    over_peers(lambda k: r_copy(k).start())
    returned[mine, :] = refined[mine, :]
    over_peers(lambda k: r_copy(k).wait())
    o_ref[...] = returned[...]


def body(
    feature_map,
    queries,
    corner,
    offsets,
    visible,
    w_embed,
    w_qkv,
    w_out,
    gain_attn,
    gain_mlp,
    w_up,
    w_down,
    w_head,
):
    n = lax.axis_size("frame")
    cells, chan = feature_map.shape[1:]
    tracks = corner.shape[1]
    rows = n * (tracks // n)
    width = w_embed.shape[1]
    anywhere = pl.BlockSpec(memory_space=pl.ANY)
    vmem = pl.BlockSpec(memory_space=pltpu.VMEM)
    smem = pl.BlockSpec(memory_space=pltpu.SMEM)
    dma = pltpu.SemaphoreType.DMA
    weights = [w_embed, w_qkv, w_out, w_up, w_down, w_head]
    first = corner // TILE
    second = (corner + GRID_W) // TILE
    last = cells // TILE - 1
    places = jnp.concatenate(
        [first, jnp.minimum(first + 1, last), second, jnp.minimum(second + 1, last)], axis=0
    )
    out = pl.pallas_call(
        functools.partial(kernel, n),
        out_shape=jax.ShapeDtypeStruct((tracks, chan), BF16),
        in_specs=[
            anywhere,
            vmem,
            smem,
            vmem,
            vmem,
            vmem,
            anywhere,
            anywhere,
            anywhere,
            vmem,
            vmem,
            anywhere,
            anywhere,
            anywhere,
        ],
        out_specs=vmem,
        scratch_shapes=[pltpu.VMEM((cells // TILE, TILE, chan), BF16)]
        + [pltpu.VMEM(w.shape, w.dtype) for w in weights]
        + [
            pltpu.VMEM((tracks, chan), BF16),
            pltpu.VMEM((n, 1, tracks), jnp.int32),
            pltpu.VMEM((tracks, 8), F32),
            pltpu.VMEM((tracks, chan), F32),
            pltpu.VMEM((tracks, width), BF16),
            pltpu.VMEM((rows, width), BF16),
            pltpu.VMEM((rows, w_qkv.shape[1]), BF16),
            pltpu.VMEM((rows, chan), BF16),
            pltpu.VMEM((tracks, chan), BF16),
            dma((5,)),
            dma((len(weights),)),
        ]
        + [dma((n,))] * 8,
        compiler_params=pltpu.CompilerParams(
            collective_id=0, has_side_effects=True, vmem_limit_bytes=48 * 1024 * 1024
        ),
    )(
        feature_map.reshape(cells // TILE, TILE, chan),
        queries,
        places,
        corner,
        offsets[0],
        visible,
        w_embed,
        w_qkv,
        w_out,
        gain_attn.reshape(1, width),
        gain_mlp.reshape(1, width),
        w_up,
        w_down,
        w_head,
    )
    return out[None]


def solution(mesh):
    split = ("clip", "frame")
    in_specs = (
        P(split, None, None),
        P(split, None),
        P(split, None),
        P(split, None, None),
        P(split, None),
    ) + (P(),) * 8
    out_specs = P(split, None, None)
    return jax.shard_map(body, mesh=mesh, in_specs=in_specs, out_specs=out_specs, check_vma=False)
```

```python
import functools
import math

import jax
import jax.numpy as jnp
from jax import lax
from jax.experimental import pallas as pl
from jax.experimental.pallas import tpu as pltpu
from jax.sharding import PartitionSpec as P

HEADS = 8
GRID_W = 120
EPS = 1e-06
TILE = 16
WINDOW = 2 * TILE
GROUP = 16
MESH = pl.DeviceIdType.MESH
F32 = jnp.float32
BF16 = jnp.bfloat16


def pick_chunk(cells, limit):
    best = 16
    for rows in range(16, limit + 1, 16):
        if cells % rows == 0:
            best = rows
    return best


def each(count, step):
    if count == 1:
        step(0)
    else:

        def looped(i, carry):
            step(i)
            return carry

        lax.fori_loop(0, count, looped, 0)


def start_of(i, size):
    if isinstance(i, int):
        return i * size
    return pl.multiple_of(i * size, size)


def rms_scale(values, gain):
    return values * lax.rsqrt(jnp.mean(values * values, axis=-1, keepdims=True) + EPS) * gain


def dot(a, b):
    return jnp.dot(a, b, preferred_element_type=F32)


def dot_nt(a, b):
    return lax.dot_general(a, b, (((1,), (1,)), ((), ())), preferred_element_type=F32)


def dot_tn(a, b):
    return lax.dot_general(a, b, (((0,), (0,)), ((), ())), preferred_element_type=F32)


def kernel(
    n,
    fm_hbm,
    q_hbm,
    corner_hbm,
    off_hbm,
    vis_hbm,
    we_hbm,
    wqkv_hbm,
    wout_hbm,
    ga_hbm,
    gm_hbm,
    wup_hbm,
    wdown_hbm,
    whead_hbm,
    o_ref,
    fm,
    we,
    wqkv,
    wout,
    wup,
    wdown,
    whead,
    ga_ref,
    gm_ref,
    corner_ref,
    off_ref,
    tiles_v,
    tiles_s,
    q_all,
    vis_all,
    table,
    sampled,
    sampled_in,
    pooled,
    pooled_in,
    bias,
    stream,
    packed,
    refined,
    returned,
    fm_sem,
    w_sem,
    in_sem,
    q_send,
    q_recv,
    v_send,
    v_recv,
    a_send,
    a_recv,
    s_send,
    s_recv,
    r_send,
    r_recv,
):
    chan = fm.shape[2]
    cells = fm.shape[0] * TILE
    tracks = q_all.shape[0]
    per = tracks // n
    rows = n * per
    width = stream.shape[1]
    me = lax.axis_index("frame")
    clip = lax.axis_index("clip")

    def peer(k):
        return lax.rem(me + k, n)

    barrier = pltpu.get_barrier_semaphore()

    def greet(k, carry):
        pl.semaphore_signal(barrier, inc=1, device_id=(clip, peer(k)), device_id_type=MESH)
        return carry

    lax.fori_loop(1, n, greet, 0)

    mine = pl.ds(pl.multiple_of(me * per, per), per)
    in_copies = [
        pltpu.make_async_copy(src, dst, in_sem.at[i])
        for i, (src, dst) in enumerate(
            [
                (q_hbm, q_all.at[mine]),
                (vis_hbm, vis_all.at[me]),
                (corner_hbm, corner_ref),
                (off_hbm, off_ref),
            ]
        )
    ]
    for copy in in_copies:
        copy.start()
    parts = fm_sem.shape[0]
    part_rows = fm.shape[0] // parts
    fm_copies = []
    for i in range(parts):
        piece = pl.ds(i * part_rows, part_rows)
        fm_copies.append(pltpu.make_async_copy(fm_hbm.at[piece], fm.at[piece], fm_sem.at[i]))
    for copy in fm_copies:
        copy.start()
    w_copies = [
        pltpu.make_async_copy(src, dst, w_sem.at[i])
        for i, (src, dst) in enumerate(
            [
                (we_hbm, we),
                (wqkv_hbm, wqkv),
                (wout_hbm, wout),
                (wup_hbm, wup),
                (wdown_hbm, wdown),
                (whead_hbm, whead),
                (ga_hbm, ga_ref),
                (gm_hbm, gm_ref),
            ]
        )
    ]
    for copy in in_copies:
        copy.wait()

    idx = corner_ref[...]
    last = fm.shape[0] - 1
    tiles_v[...] = jnp.concatenate(
        [
            idx // TILE,
            jnp.minimum(idx // TILE + 1, last),
            (idx + GRID_W) // TILE,
            jnp.minimum((idx + GRID_W) // TILE + 1, last),
        ],
        axis=0,
    )
    tiles_copy = pltpu.make_async_copy(tiles_v, tiles_s, in_sem.at[4])
    tiles_copy.start()
    pl.semaphore_wait(barrier, n - 1)

    def q_copy(k):
        return pltpu.make_async_remote_copy(
            src_ref=q_all.at[mine],
            dst_ref=q_all.at[mine],
            send_sem=q_send.at[k],
            recv_sem=q_recv.at[k],
            device_id=(clip, peer(k)),
            device_id_type=MESH,
        )

    def v_copy(k):
        return pltpu.make_async_remote_copy(
            src_ref=vis_all.at[me],
            dst_ref=vis_all.at[me],
            send_sem=v_send.at[k],
            recv_sem=v_recv.at[k],
            device_id=(clip, peer(k)),
            device_id_type=MESH,
        )

    def exchange(src, dst, send, recv):
        def copy(k):
            other = peer(k)
            return pltpu.make_async_remote_copy(
                src_ref=src.at[pl.ds(pl.multiple_of(other * per, per), per)],
                dst_ref=dst.at[mine],
                send_sem=send.at[k],
                recv_sem=recv.at[k],
                device_id=(clip, other),
                device_id_type=MESH,
            )

        return copy

    a_copy = exchange(sampled, sampled_in, a_send, a_recv)
    s_copy = exchange(pooled, pooled_in, s_send, s_recv)
    r_copy = exchange(refined, returned, r_send, r_recv)

    def over_peers(action):
        def step(k, carry):
            action(k)
            return carry

        lax.fori_loop(1, n, step, 0)

    over_peers(lambda k: q_copy(k).start())
    over_peers(lambda k: v_copy(k).start())

    ox = off_ref[0:1, :]
    oy = off_ref[1:2, :]
    table[...] = jnp.concatenate(
        [
            (idx % TILE).astype(F32),
            ((idx + GRID_W) % TILE + WINDOW).astype(F32),
            (1.0 - ox) * (1.0 - oy),
            ox * (1.0 - oy),
            (1.0 - ox) * oy,
            ox * oy,
            ox,
            oy,
        ],
        axis=0,
    ).T
    tiles_copy.wait()
    for copy in fm_copies:
        copy.wait()
    for copy in w_copies:
        copy.start()

    span = 2 * WINDOW
    lane = lax.broadcasted_iota(jnp.int32, (GROUP, GROUP * span), 1)
    own = lane // span == lax.broadcasted_iota(jnp.int32, (GROUP, GROUP * span), 0)
    within = jnp.where(own, lane % span, -2).astype(F32)

    def sample(g, carry):
        first = pl.multiple_of(g * GROUP, GROUP)
        pieces = []
        for t in range(GROUP):
            for i in range(4):
                pieces.append(fm[tiles_s[i, first + t]])
        window = jnp.concatenate(pieces, axis=0)
        facts = table[pl.ds(first, GROUP), :]
        p = facts[:, 0:1]
        r = facts[:, 1:2]
        zero = jnp.zeros_like(within)
        weight = jnp.where(within == p, facts[:, 2:3], zero)
        weight = jnp.where(within == p + 1.0, facts[:, 3:4], weight)
        weight = jnp.where(within == r, facts[:, 4:5], weight)
        weight = jnp.where(within == r + 1.0, facts[:, 5:6], weight)
        coarse = weight.astype(BF16)
        fine = (weight - coarse.astype(F32)).astype(BF16)
        both = dot(jnp.concatenate([coarse, fine], axis=0), window)
        sampled[pl.ds(first, GROUP), :] = (both[:GROUP] + both[GROUP:]).astype(BF16)
        return carry

    lax.fori_loop(0, tracks // GROUP, sample, 0, unroll=2)
    over_peers(lambda k: a_copy(k).start())
    sampled_in[mine, :] = sampled[mine, :]

    over_peers(lambda k: q_copy(k).wait())

    block = math.gcd(tracks, 256)
    chunk = pick_chunk(cells, 1100)
    chunks = cells // chunk
    factor = math.log2(math.e) / math.sqrt(chan)

    def correlate(b):
        here = pl.ds(start_of(b, block), block)
        q = q_all[here, :]

        def piece_of(c):
            return fm[pl.ds(c * (chunk // TILE), chunk // TILE)].reshape(chunk, chan)

        def scores(c):
            return dot_nt(piece_of(c), q)

        ahead = scores(0)
        peak = total = acc = None
        for c in range(chunks):
            s = ahead
            if c + 1 < chunks:
                ahead = scores(c + 1)
            high = jnp.max(s, axis=0, keepdims=True)
            new = high if peak is None else jnp.maximum(peak, high)
            p = jnp.exp2(s * factor - new * factor)
            mass = jnp.sum(p, axis=0, keepdims=True)
            part = dot_tn(piece_of(c), p.astype(BF16))
            if peak is None:
                total, acc = mass, part
            else:
                shrink = jnp.exp2((peak - new) * factor)
                total = total * shrink + mass
                acc = acc * shrink + part
            peak = new
        pooled[here, :] = (acc / total).T.astype(BF16)

    each(tracks // block, correlate)

    over_peers(lambda k: s_copy(k).start())
    pooled_in[mine, :] = pooled[mine, :]

    over_peers(lambda k: v_copy(k).wait())
    shown = vis_all[...].reshape(n, tracks).astype(F32).astype(BF16)
    tall = lax.broadcasted_iota(jnp.int32, (tracks, rows), 0)
    wide = lax.broadcasted_iota(jnp.int32, (tracks, rows), 1)
    pick = jnp.where(tall == me * per + wide % per, 1.0, 0.0).astype(BF16)
    frame_row = lax.broadcasted_iota(jnp.int32, (n, rows), 0)
    frame_col = lax.broadcasted_iota(jnp.int32, (n, rows), 1) // per
    seen = jnp.sum(
        jnp.where(frame_row == frame_col, dot(shown, pick), 0.0), axis=0, keepdims=True
    )
    piece = math.gcd(rows, 256)

    def mask(b):
        first = start_of(b, piece)
        q_row = lax.broadcasted_iota(jnp.int32, (piece, rows), 0) + first
        k_row = lax.broadcasted_iota(jnp.int32, (piece, rows), 1)
        same = q_row % per == k_row % per
        keep = jnp.logical_and(same, jnp.logical_or(q_row == k_row, seen > 0.5))
        bias[pl.ds(first, piece), :] = jnp.where(keep, 0.0, -1e30)

    each(rows // piece, mask)
    for copy in w_copies:
        copy.wait()
    over_peers(lambda k: a_copy(k).wait())
    over_peers(lambda k: s_copy(k).wait())

    def project(b):
        here = pl.ds(start_of(b, piece), piece)
        token = jnp.concatenate([sampled_in[here, :], pooled_in[here, :]], axis=1)
        embedded = dot(token, we[...]).astype(BF16)
        stream[here, :] = embedded
        normed = rms_scale(embedded.astype(F32), ga_ref[...][None, :]).astype(BF16)
        packed[here, :] = dot(normed, wqkv[...]).astype(BF16)

    each(rows // piece, project)

    size = width // HEADS

    def refine(b):
        first = start_of(b, piece)
        here = pl.ds(first, piece)
        off = bias[here, :]
        tiles = [None] * (width // 128)
        for h in range(HEADS):
            lo = h * size // 128
            hi = -(-(h + 1) * size // 128)
            cols = lax.broadcasted_iota(jnp.int32, (1, (hi - lo) * 128), 1) + lo * 128
            inside = jnp.logical_and(cols >= h * size, cols < (h + 1) * size)
            gate = jnp.where(inside, 1.0, 0.0)
            qh = packed[here, lo * 128 : hi * 128] * gate.astype(BF16)
            kh = packed[:, width + lo * 128 : width + hi * 128]
            vh = packed[:, 2 * width + lo * 128 : 2 * width + hi * 128]
            s = dot_nt(qh, kh) * (1.0 / math.sqrt(size)) + off
            p = jnp.exp(s - jnp.max(s, axis=1, keepdims=True))
            attn = (p / jnp.sum(p, axis=1, keepdims=True)).astype(BF16)
            got = dot(attn, vh) * gate
            for i in range(lo, hi):
                add = got[:, (i - lo) * 128 : (i - lo + 1) * 128]
                tiles[i] = add if tiles[i] is None else tiles[i] + add
        context = jnp.concatenate(tiles, axis=1).astype(BF16)
        mixed = stream[here, :].astype(F32) + dot(context, wout[...])
        normed = rms_scale(mixed, gm_ref[...][None, :]).astype(BF16)
        hidden = jax.nn.gelu(dot(normed, wup[...])).astype(BF16)
        final = (mixed + dot(hidden, wdown[...])).astype(BF16)
        refined[here, :] = dot(final, whead[...]).astype(BF16)

    each(rows // piece, refine)

    over_peers(lambda k: r_copy(k).start())
    returned[mine, :] = refined[mine, :]
    over_peers(lambda k: r_copy(k).wait())
    o_ref[...] = returned[...]


def body(
    feature_map,
    queries,
    corner,
    offsets,
    visible,
    w_embed,
    w_qkv,
    w_out,
    gain_attn,
    gain_mlp,
    w_up,
    w_down,
    w_head,
):
    n = lax.axis_size("frame")
    cells, chan = feature_map.shape[1:]
    tracks = corner.shape[1]
    rows = n * (tracks // n)
    width = w_embed.shape[1]
    hbm = pl.BlockSpec(memory_space=pltpu.HBM)
    vmem = pl.BlockSpec(memory_space=pltpu.VMEM)
    dma = pltpu.SemaphoreType.DMA
    weights = [w_embed, w_qkv, w_out, w_up, w_down, w_head, gain_attn, gain_mlp]
    out = pl.pallas_call(
        functools.partial(kernel, n),
        out_shape=jax.ShapeDtypeStruct((tracks, chan), BF16),
        in_specs=[hbm] * 13,
        out_specs=vmem,
        scratch_shapes=[pltpu.VMEM((cells // TILE, TILE, chan), BF16)]
        + [pltpu.VMEM(w.shape, w.dtype) for w in weights]
        + [
            pltpu.VMEM(corner.shape, jnp.int32),
            pltpu.VMEM(offsets.shape[1:], F32),
            pltpu.VMEM((4, tracks), jnp.int32),
            pltpu.SMEM((4, tracks), jnp.int32),
            pltpu.VMEM((tracks, chan), BF16),
            pltpu.VMEM((n, 1, tracks), jnp.int32),
            pltpu.VMEM((tracks, 8), F32),
            pltpu.VMEM((tracks, chan), BF16),
            pltpu.VMEM((rows, chan), BF16),
            pltpu.VMEM((tracks, chan), BF16),
            pltpu.VMEM((rows, chan), BF16),
            pltpu.VMEM((rows, rows), F32),
            pltpu.VMEM((rows, width), BF16),
            pltpu.VMEM((rows, w_qkv.shape[1]), BF16),
            pltpu.VMEM((rows, chan), BF16),
            pltpu.VMEM((tracks, chan), BF16),
            dma((5,)),
            dma((len(weights),)),
            dma((5,)),
        ]
        + [dma((n,))] * 10,
        compiler_params=pltpu.CompilerParams(
            collective_id=0, has_side_effects=True, vmem_limit_bytes=60 * 1024 * 1024
        ),
    )(
        feature_map.reshape(cells // TILE, TILE, chan),
        queries,
        corner,
        offsets[0],
        visible,
        w_embed,
        w_qkv,
        w_out,
        gain_attn,
        gain_mlp,
        w_up,
        w_down,
        w_head,
    )
    return out[None]


def solution(mesh):
    split = ("clip", "frame")
    in_specs = (
        P(split, None, None),
        P(split, None),
        P(split, None),
        P(split, None, None),
        P(split, None),
    ) + (P(),) * 8
    out_specs = P(split, None, None)
    return jax.shard_map(body, mesh=mesh, in_specs=in_specs, out_specs=out_specs, check_vma=False)
```

```python
import functools
import math

import jax
import jax.numpy as jnp
from jax import lax
from jax.experimental import pallas as pl
from jax.experimental.pallas import tpu as pltpu
from jax.sharding import PartitionSpec as P

HEADS = 8
GRID_W = 120
EPS = 1e-06
TILE = 16
WINDOW = 2 * TILE
GROUP = 16
MESH = pl.DeviceIdType.MESH
F32 = jnp.float32
BF16 = jnp.bfloat16


def pick_chunk(cells, limit):
    best = 16
    for rows in range(16, limit + 1, 16):
        if cells % rows == 0:
            best = rows
    return best


def each(count, step):
    if count == 1:
        step(0)
    else:

        def looped(i, carry):
            step(i)
            return carry

        lax.fori_loop(0, count, looped, 0)


def start_of(i, size):
    if isinstance(i, int):
        return i * size
    return pl.multiple_of(i * size, size)


def rms_scale(values, gain):
    return values * lax.rsqrt(jnp.mean(values * values, axis=-1, keepdims=True) + EPS) * gain


def dot(a, b):
    return jnp.dot(a, b, preferred_element_type=F32)


def dot_nt(a, b):
    return lax.dot_general(a, b, (((1,), (1,)), ((), ())), preferred_element_type=F32)


def dot_tn(a, b):
    return lax.dot_general(a, b, (((0,), (0,)), ((), ())), preferred_element_type=F32)


def kernel(
    n,
    fm_hbm,
    q_hbm,
    corner_hbm,
    off_hbm,
    vis_hbm,
    we_hbm,
    wqkv_hbm,
    wout_hbm,
    ga_hbm,
    gm_hbm,
    wup_hbm,
    wdown_hbm,
    whead_hbm,
    o_ref,
    fm,
    we,
    wqkv,
    wout,
    wup,
    wdown,
    whead,
    ga_ref,
    gm_ref,
    corner_ref,
    off_ref,
    tiles_v,
    tiles_s,
    q_all,
    vis_all,
    table,
    sampled,
    sampled_in,
    pooled,
    pooled_in,
    bias,
    stream,
    packed,
    refined,
    fm_sem,
    w_sem,
    in_sem,
    q_send,
    q_recv,
    v_send,
    v_recv,
    a_send,
    a_recv,
    s_send,
    s_recv,
    r_send,
    r_recv,
):
    chan = fm.shape[2]
    cells = fm.shape[0] * TILE
    tracks = q_all.shape[0]
    per = tracks // n
    rows = n * per
    width = stream.shape[1]
    me = lax.axis_index("frame")
    clip = lax.axis_index("clip")

    def peer(k):
        return lax.rem(me + k, n)

    barrier = pltpu.get_barrier_semaphore()

    def greet(k, carry):
        pl.semaphore_signal(barrier, inc=1, device_id=(clip, peer(k)), device_id_type=MESH)
        return carry

    lax.fori_loop(1, n, greet, 0)

    mine = pl.ds(pl.multiple_of(me * per, per), per)
    in_copies = [
        pltpu.make_async_copy(src, dst, in_sem.at[i])
        for i, (src, dst) in enumerate(
            [
                (q_hbm, q_all.at[mine]),
                (vis_hbm, vis_all.at[me]),
                (corner_hbm, corner_ref),
                (off_hbm, off_ref),
            ]
        )
    ]
    for copy in in_copies:
        copy.start()
    parts = fm_sem.shape[0]
    part_rows = fm.shape[0] // parts
    fm_copies = []
    for i in range(parts):
        piece = pl.ds(i * part_rows, part_rows)
        fm_copies.append(pltpu.make_async_copy(fm_hbm.at[piece], fm.at[piece], fm_sem.at[i]))
    for copy in fm_copies:
        copy.start()
    w_copies = [
        pltpu.make_async_copy(src, dst, w_sem.at[i])
        for i, (src, dst) in enumerate(
            [
                (we_hbm, we),
                (wqkv_hbm, wqkv),
                (wout_hbm, wout),
                (wup_hbm, wup),
                (wdown_hbm, wdown),
                (whead_hbm, whead),
                (ga_hbm, ga_ref),
                (gm_hbm, gm_ref),
            ]
        )
    ]
    for copy in in_copies:
        copy.wait()

    idx = corner_ref[...]
    last = fm.shape[0] - 1
    tiles_v[...] = jnp.concatenate(
        [
            idx // TILE,
            jnp.minimum(idx // TILE + 1, last),
            (idx + GRID_W) // TILE,
            jnp.minimum((idx + GRID_W) // TILE + 1, last),
        ],
        axis=0,
    )
    tiles_copy = pltpu.make_async_copy(tiles_v, tiles_s, in_sem.at[4])
    tiles_copy.start()
    pl.semaphore_wait(barrier, n - 1)

    def q_copy(k):
        return pltpu.make_async_remote_copy(
            src_ref=q_all.at[mine],
            dst_ref=q_all.at[mine],
            send_sem=q_send.at[k],
            recv_sem=q_recv.at[k],
            device_id=(clip, peer(k)),
            device_id_type=MESH,
        )

    def v_copy(k):
        return pltpu.make_async_remote_copy(
            src_ref=vis_all.at[me],
            dst_ref=vis_all.at[me],
            send_sem=v_send.at[k],
            recv_sem=v_recv.at[k],
            device_id=(clip, peer(k)),
            device_id_type=MESH,
        )

    def exchange(src, dst, send, recv):
        def copy(k):
            other = peer(k)
            return pltpu.make_async_remote_copy(
                src_ref=src.at[pl.ds(pl.multiple_of(other * per, per), per)],
                dst_ref=dst.at[mine],
                send_sem=send.at[k],
                recv_sem=recv.at[k],
                device_id=(clip, other),
                device_id_type=MESH,
            )

        return copy

    a_copy = exchange(sampled, sampled_in, a_send, a_recv)
    s_copy = exchange(pooled, pooled_in, s_send, s_recv)
    r_copy = exchange(refined, o_ref, r_send, r_recv)

    def over_peers(action):
        def step(k, carry):
            action(k)
            return carry

        lax.fori_loop(1, n, step, 0, unroll=5)

    over_peers(lambda k: q_copy(k).start())
    over_peers(lambda k: v_copy(k).start())

    ox = off_ref[0:1, :]
    oy = off_ref[1:2, :]
    table[...] = jnp.concatenate(
        [
            (idx % TILE).astype(F32),
            ((idx + GRID_W) % TILE + WINDOW).astype(F32),
            (1.0 - ox) * (1.0 - oy),
            ox * (1.0 - oy),
            (1.0 - ox) * oy,
            ox * oy,
            ox,
            oy,
        ],
        axis=0,
    ).T
    tiles_copy.wait()
    for copy in fm_copies:
        copy.wait()
    for copy in w_copies:
        copy.start()

    span = 2 * WINDOW
    lane = lax.broadcasted_iota(jnp.int32, (GROUP, GROUP * span), 1)
    own = lane // span == lax.broadcasted_iota(jnp.int32, (GROUP, GROUP * span), 0)
    within = jnp.where(own, lane % span, -2).astype(F32)

    def sample(g, carry):
        first = pl.multiple_of(g * GROUP, GROUP)
        pieces = []
        for t in range(GROUP):
            for i in range(4):
                pieces.append(fm[tiles_s[i, first + t]])
        window = jnp.concatenate(pieces, axis=0)
        facts = table[pl.ds(first, GROUP), :]
        p = facts[:, 0:1]
        r = facts[:, 1:2]
        zero = jnp.zeros_like(within)
        weight = jnp.where(within == p, facts[:, 2:3], zero)
        weight = jnp.where(within == p + 1.0, facts[:, 3:4], weight)
        weight = jnp.where(within == r, facts[:, 4:5], weight)
        weight = jnp.where(within == r + 1.0, facts[:, 5:6], weight)
        coarse = weight.astype(BF16)
        fine = (weight - coarse.astype(F32)).astype(BF16)
        both = dot(jnp.concatenate([coarse, fine], axis=0), window)
        sampled[pl.ds(first, GROUP), :] = (both[:GROUP] + both[GROUP:]).astype(BF16)
        return carry

    lax.fori_loop(0, tracks // GROUP, sample, 0, unroll=2)
    over_peers(lambda k: a_copy(k).start())
    sampled_in[mine, :] = sampled[mine, :]

    over_peers(lambda k: q_copy(k).wait_recv())

    block = math.gcd(tracks, 256)
    chunk = pick_chunk(cells, 2720)
    chunks = cells // chunk
    factor = math.log2(math.e) / math.sqrt(chan)

    def correlate(b):
        here = pl.ds(start_of(b, block), block)
        q = q_all[here, :]

        def piece_of(c):
            return fm[pl.ds(c * (chunk // TILE), chunk // TILE)].reshape(chunk, chan)

        def scores(c):
            return dot_nt(piece_of(c), q)

        ahead = scores(0)
        peak = total = acc = None
        for c in range(chunks):
            s = ahead
            if c + 1 < chunks:
                ahead = scores(c + 1)
            high = jnp.max(s, axis=0, keepdims=True)
            new = high if peak is None else jnp.maximum(peak, high)
            p = jnp.exp2(s * factor - new * factor)
            mass = jnp.sum(p, axis=0, keepdims=True)
            part = dot_tn(piece_of(c), p.astype(BF16))
            if peak is None:
                total, acc = mass, part
            else:
                shrink = jnp.exp2((peak - new) * factor)
                total = total * shrink + mass
                acc = acc * shrink + part
            peak = new
        pooled[here, :] = (acc / total).T.astype(BF16)

    each(tracks // block, correlate)

    over_peers(lambda k: s_copy(k).start())
    pooled_in[mine, :] = pooled[mine, :]

    over_peers(lambda k: v_copy(k).wait_recv())
    shown = vis_all[...].reshape(n, tracks).astype(F32).astype(BF16)
    tall = lax.broadcasted_iota(jnp.int32, (tracks, rows), 0)
    wide = lax.broadcasted_iota(jnp.int32, (tracks, rows), 1)
    pick = jnp.where(tall == me * per + wide % per, 1.0, 0.0).astype(BF16)
    frame_row = lax.broadcasted_iota(jnp.int32, (n, rows), 0)
    frame_col = lax.broadcasted_iota(jnp.int32, (n, rows), 1) // per
    seen = jnp.sum(
        jnp.where(frame_row == frame_col, dot(shown, pick), 0.0), axis=0, keepdims=True
    )
    piece = math.gcd(rows, 256)

    def mask(b):
        first = start_of(b, piece)
        q_row = lax.broadcasted_iota(jnp.int32, (piece, rows), 0) + first
        k_row = lax.broadcasted_iota(jnp.int32, (piece, rows), 1)
        same = q_row % per == k_row % per
        keep = jnp.logical_and(same, jnp.logical_or(q_row == k_row, seen > 0.5))
        bias[pl.ds(first, piece), :] = jnp.where(keep, 0.0, -1e30)

    each(rows // piece, mask)
    for copy in w_copies:
        copy.wait()
    over_peers(lambda k: a_copy(k).wait_recv())
    over_peers(lambda k: s_copy(k).wait_recv())

    def project(b):
        here = pl.ds(start_of(b, piece), piece)
        token = jnp.concatenate([sampled_in[here, :], pooled_in[here, :]], axis=1)
        embedded = dot(token, we[...]).astype(BF16)
        stream[here, :] = embedded
        normed = rms_scale(embedded.astype(F32), ga_ref[...][None, :]).astype(BF16)
        packed[here, :] = dot(normed, wqkv[...]).astype(BF16)

    each(rows // piece, project)

    size = width // HEADS

    def refine(b):
        first = start_of(b, piece)
        here = pl.ds(first, piece)
        off = bias[here, :]
        tiles = [None] * (width // 128)
        for h in range(HEADS):
            lo = h * size // 128
            hi = -(-(h + 1) * size // 128)
            cols = lax.broadcasted_iota(jnp.int32, (1, (hi - lo) * 128), 1) + lo * 128
            inside = jnp.logical_and(cols >= h * size, cols < (h + 1) * size)
            gate = jnp.where(inside, 1.0, 0.0)
            qh = packed[here, lo * 128 : hi * 128] * gate.astype(BF16)
            kh = packed[:, width + lo * 128 : width + hi * 128]
            vh = packed[:, 2 * width + lo * 128 : 2 * width + hi * 128]
            s = dot_nt(qh, kh) * (1.0 / math.sqrt(size)) + off
            p = jnp.exp(s - jnp.max(s, axis=1, keepdims=True))
            attn = (p / jnp.sum(p, axis=1, keepdims=True)).astype(BF16)
            got = dot(attn, vh) * gate
            for i in range(lo, hi):
                add = got[:, (i - lo) * 128 : (i - lo + 1) * 128]
                tiles[i] = add if tiles[i] is None else tiles[i] + add
        context = jnp.concatenate(tiles, axis=1).astype(BF16)
        mixed = stream[here, :].astype(F32) + dot(context, wout[...])
        normed = rms_scale(mixed, gm_ref[...][None, :]).astype(BF16)
        hidden = jax.nn.gelu(dot(normed, wup[...])).astype(BF16)
        final = (mixed + dot(hidden, wdown[...])).astype(BF16)
        refined[here, :] = dot(final, whead[...]).astype(BF16)

    each(rows // piece, refine)

    over_peers(lambda k: r_copy(k).start())
    kept = pltpu.make_async_copy(refined.at[mine], o_ref.at[mine], in_sem.at[5])
    kept.start()
    over_peers(lambda k: r_copy(k).wait_recv())
    kept.wait()
    for copy in (q_copy, v_copy, a_copy, s_copy, r_copy):
        over_peers(lambda k: copy(k).wait_send())


def body(
    feature_map,
    queries,
    corner,
    offsets,
    visible,
    w_embed,
    w_qkv,
    w_out,
    gain_attn,
    gain_mlp,
    w_up,
    w_down,
    w_head,
):
    n = lax.axis_size("frame")
    cells, chan = feature_map.shape[1:]
    tracks = corner.shape[1]
    rows = n * (tracks // n)
    width = w_embed.shape[1]
    hbm = pl.BlockSpec(memory_space=pltpu.HBM)
    dma = pltpu.SemaphoreType.DMA
    weights = [w_embed, w_qkv, w_out, w_up, w_down, w_head, gain_attn, gain_mlp]
    out = pl.pallas_call(
        functools.partial(kernel, n),
        out_shape=jax.ShapeDtypeStruct((tracks, chan), BF16),
        in_specs=[hbm] * 13,
        out_specs=hbm,
        scratch_shapes=[pltpu.VMEM((cells // TILE, TILE, chan), BF16)]
        + [pltpu.VMEM(w.shape, w.dtype) for w in weights]
        + [
            pltpu.VMEM(corner.shape, jnp.int32),
            pltpu.VMEM(offsets.shape[1:], F32),
            pltpu.VMEM((4, tracks), jnp.int32),
            pltpu.SMEM((4, tracks), jnp.int32),
            pltpu.VMEM((tracks, chan), BF16),
            pltpu.VMEM((n, 1, tracks), jnp.int32),
            pltpu.VMEM((tracks, 8), F32),
            pltpu.VMEM((tracks, chan), BF16),
            pltpu.VMEM((rows, chan), BF16),
            pltpu.VMEM((tracks, chan), BF16),
            pltpu.VMEM((rows, chan), BF16),
            pltpu.VMEM((rows, rows), F32),
            pltpu.VMEM((rows, width), BF16),
            pltpu.VMEM((rows, w_qkv.shape[1]), BF16),
            pltpu.VMEM((rows, chan), BF16),
            dma((5,)),
            dma((len(weights),)),
            dma((6,)),
        ]
        + [dma((n,))] * 10,
        compiler_params=pltpu.CompilerParams(
            collective_id=0, has_side_effects=True, vmem_limit_bytes=60 * 1024 * 1024
        ),
    )(
        feature_map.reshape(cells // TILE, TILE, chan),
        queries,
        corner,
        offsets[0],
        visible,
        w_embed,
        w_qkv,
        w_out,
        gain_attn,
        gain_mlp,
        w_up,
        w_down,
        w_head,
    )
    return out[None]


def solution(mesh):
    split = ("clip", "frame")
    in_specs = (
        P(split, None, None),
        P(split, None),
        P(split, None),
        P(split, None, None),
        P(split, None),
    ) + (P(),) * 8
    out_specs = P(split, None, None)
    return jax.shard_map(body, mesh=mesh, in_specs=in_specs, out_specs=out_specs, check_vma=False)
```
